256 devices in a mesh: row: 16 (over y_hi, z), col: 16 (over y_lo, x, core).
Axes of the slice: x: 4, y: 4 (y_hi: 2, y_lo: 2; y = y_hi * 2 + y_lo), z: 8, core: 2. Of those that a mesh axis runs over, the one named last changes fastest.
Arguments:
- ancestor: bfloat16 [16384, 16384], P('row', 'col'), may hold values from -6 to 6
- lblocks: bfloat16 [16, 6, 256, 256], P('col'), may hold values from -0.15234375 to 0.15234375
- lrows: int32 [16, 6], replicated, may hold values from 0 to 63, as said below
- dinv: float32 [16, 256, 256], P('col'), may hold values from -6 to 6
Outputs:
- inverse_panel: bfloat16 [16, 16384, 256], P('col', 'row')
- diagonal_block: float32 [16, 256, 256], P('col')
The draws below stay inside these ranges and needn't reach their ends.
Inputs may be any that keep to these rules, and one draw needn't show every extreme that they name: `lrows`: each supernode lists 6 different block rows; for every c, block rows c * 4 to (c + 1) * 4 - 1 are listed at most 6 times over all supernodes and at most 1 times by one supernode, and both bounds are reached.
All inputs are finite; a program needn't handle non-finite values.
Results may differ from the reference program's by a relative error of at most 0.018.
Values may be sent and summed in bfloat16 or wider, within the bound.
A program may use at most 128 MiB of HBM per device.

```python
import jax
import jax.numpy as jnp
from jax import lax

S = 256
NL = 6
NB = 64
G = 16
N_COL = 16


def draw_lrows(key, part):
    key = jax.random.fold_in(key, 5)
    col_blocks = NB // N_COL
    shift = jax.random.randint(jax.random.fold_in(key, 1), (), 0, N_COL)
    flat = jnp.arange(G * NL, dtype=jnp.int32).reshape(G, NL)
    device = (flat + shift) % N_COL
    base = jax.random.randint(jax.random.fold_in(key, 2), (G, N_COL), 0, col_blocks)
    start = jnp.take_along_axis(base, device, axis=1)
    offset = (start + jnp.arange(NL, dtype=jnp.int32)[None, :] // N_COL) % col_blocks
    listing = device * col_blocks + offset
    order = jax.random.permutation(jax.random.fold_in(key, 3), G)
    return listing[order].astype(jnp.int32)


def block_levels(rng, extent, cuts, least, largest):
    gain, own = 1.0, jax.random.fold_in(rng, 6)
    for axis_at, parts in cuts:
        draws = jnp.exp(jax.random.uniform(jax.random.fold_in(own, axis_at), (parts,), jnp.float32, least / len(cuts), largest / len(cuts)))
        gain = gain * jnp.repeat(draws, extent[axis_at] // parts).reshape([-1 if axis == axis_at else 1 for axis in range(len(extent))])
    return gain


def normal_values(rng, shape, deviation, bound, shards=(), kind=jnp.bfloat16):
    array = deviation * jax.random.normal(rng, shape, jnp.float32)
    if shards:
        array = array * block_levels(rng, shape, shards, -0.22, 0.18)
    return jnp.clip(array, -bound, bound).astype(kind)


def setup_inputs(seed: int = 0) -> dict:
    splits = jax.random.split(jax.random.key(seed), 5)
    ancestor = normal_values(splits[0], (NB * S, NB * S), 1.0, 6.0, ((0, 16), (1, 16)))
    lblocks = normal_values(splits[1], (G, NL, S, S), ((NL * S) ** -0.5), 0.15234375, ((0, 16),))
    lrows = draw_lrows(jax.random.fold_in(splits[4], 71), 0)
    dinv = normal_values(splits[3], (G, S, S), 1.0, 6.0, ((0, 16),), jnp.float32)
    return dict(ancestor=ancestor, lblocks=lblocks, lrows=lrows, dinv=dinv)


def reference(ancestor, lblocks, lrows, dinv):
    block_width = lblocks.shape[-1]
    matrix_order = ancestor.shape[0]
    per_column = matrix_order // block_width // N_COL

    def per_node(node_item):
        node_blocks, node_rows, node_inverse = node_item

        def add_block(totals, item_pair):
            l_block, block_index = item_pair
            first_col = (block_index * block_width).astype(jnp.int32)
            columns = lax.dynamic_slice_in_dim(ancestor, first_col, block_width, 1)
            product = jnp.dot(columns, l_block, preferred_element_type=jnp.float32)
            owner = (block_index // per_column).astype(jnp.int32)
            current = lax.dynamic_index_in_dim(totals, owner, 0, keepdims=False)
            return lax.dynamic_update_index_in_dim(totals, current + product, owner, 0), None

        initial = jnp.zeros((N_COL, matrix_order, block_width), jnp.float32)
        totals, _ = lax.scan(add_block, initial, (node_blocks, node_rows))
        rounded = lax.optimization_barrier((-totals).astype(jnp.bfloat16))
        panel_block = jnp.sum(rounded.astype(jnp.float32), axis=0).astype(jnp.bfloat16)

        def add_term(quadratic, item_pair):
            l_block, block_index = item_pair
            first_row = (block_index * block_width).astype(jnp.int32)
            panel_rows = lax.dynamic_slice_in_dim(panel_block, first_row, block_width, 0)
            return quadratic + jnp.dot(l_block.T, panel_rows, preferred_element_type=jnp.float32), None

        quadratic, _ = lax.scan(add_term, jnp.zeros((block_width, block_width), jnp.float32), (node_blocks, node_rows))
        return panel_block, node_inverse - quadratic

    inverse_panel, diagonal_block = lax.map(per_node, (lblocks, lrows, dinv))
    return inverse_panel, diagonal_block
```

```python
import functools

import jax
import jax.numpy as jnp
from jax import lax
from jax.experimental import pallas as pl
from jax.experimental.pallas import tpu as pltpu
from jax.sharding import PartitionSpec as P

MESH = pl.DeviceIdType.MESH
F32 = jnp.float32
BF16 = jnp.bfloat16

XF = (0, 1)
YF = (2, 3)


def kernel(
    lrows, anc, lb, panel, dsum,
    lin, a_own, a_sib, l0, l1, own, sb, rb0, rb1,
    x_ref, xs, ys, r1, r2, ry, ryf, ra, rbx, fin, cb, rd, dpart, ro,
    jt, slot_own, w_own, slot_sib, w_sib, rot, gsel,
    loc_sem, a_send, a_recv, t_send, t_recv0, t_recv1, g_send, g_recv,
    x_send, x_recv, d_send, d_recv,
):
    row = lax.axis_index("row")
    col = lax.axis_index("col")
    yh, z = row // 8, row % 8
    yl, x, k = col // 8, (col // 2) % 4, col % 2
    part = z % 4
    lbuf = (l0, l1)
    rbuf = (rb0, rb1)
    t_recv = (t_recv0, t_recv1)

    def at_col(y_, x_, k_):
        return (row, y_ * 8 + x_ * 2 + k_)

    def at_z(dz):
        return (yh * 8 + (z + dz + 8) % 8, col)

    xp, xm, x2 = (x + 1) % 4, (x + 3) % 4, (x + 2) % 4
    sib = at_col(yl, x, 1 - k)
    to_y = at_col(1 - yl, x, k)
    to_xp = at_col(yl, xp, k)
    to_xm = at_col(yl, xm, k)

    def remote(src, dst, send, recv, dev):
        return pltpu.make_async_remote_copy(
            src_ref=src, dst_ref=dst, send_sem=send, recv_sem=recv,
            device_id=dev, device_id_type=MESH,
        )

    lin[6] = jnp.zeros((256, 256), BF16)
    for h in range(2):
        for s in range(2):
            lbuf[h][s, :, 6] = jnp.zeros((4, 64, 128), BF16)

    ld_l = pltpu.make_async_copy(lb, lin.at[pl.ds(0, 6)], loc_sem.at[0])
    ld_l.start()
    ld_a = []
    for w in range(4):
        cp = pltpu.make_async_copy(
            anc.at[:, :, pl.ds(256 * w, 256)], a_own.at[w], loc_sem.at[1 + w]
        )
        cp.start()
        ld_a.append(cp)

    barrier = pltpu.get_barrier_semaphore()

    def greet(n, _):
        pl.semaphore_signal(barrier, inc=1, device_id=(row, (col + n) % 16), device_id_type=MESH)
        pl.semaphore_signal(barrier, inc=1, device_id=((row + n) % 16, col), device_id_type=MESH)
        return 0

    lax.fori_loop(1, 16, greet, 0)

    def find(g, owner):
        hit = jnp.int32(0)
        j_at = jnp.int32(0)
        within = jnp.int32(0)
        for j in range(6):
            v = lrows[j, g]
            eq = (v >> 2) == owner
            hit = jnp.where(eq, 1, hit)
            j_at = jnp.where(eq, j, j_at)
            within = jnp.where(eq, v & 3, within)
        return hit, j_at, within

    def table_j(c, _):
        jt[c] = find(col, c)[1]
        return 0

    lax.fori_loop(0, 16, table_j, 0)
    pl.semaphore_wait(barrier, 30)

    cp_a = []
    for w in range(4):
        cp = remote(
            anc.at[:, :, pl.ds(256 * w, 256)], a_sib.at[w], a_send.at[w], a_recv.at[w], sib
        )
        cp.start()
        cp_a.append(cp)

    ld_l.wait()
    rows_p = pl.ds(pl.multiple_of(part * 64, 64), 64)

    def a2a(h, n):
        c = (col + n) % 16
        return remote(
            sb.at[h, c], rbuf[h].at[col], t_send.at[h, n], t_recv[h].at[n], (row, c)
        )

    def a2a_in(h, n):
        c = (col - n + 16) % 16
        return remote(
            sb.at[h, c], rbuf[h].at[c], t_send.at[h, n], t_recv[h].at[n], (row, c)
        )

    for h in range(2):
        def pick(c, _, h=h):
            sb[h, c] = lin[jt[c], rows_p, pl.ds(128 * h, 128)]
            return 0

        lax.fori_loop(0, 16, pick, 0)

        def send(n, _, h=h):
            a2a(h, n).start()
            return 0

        lax.fori_loop(1, 16, send, 0)

    sib_col = col + 1 - 2 * k

    def table_g(g, carry):
        n_own, n_sib, picks = carry
        hit, _, within = find(g, col)
        slot_own[g] = jnp.where(hit == 1, jnp.minimum(n_own, 6), 6)
        w_own[g] = within
        picks = tuple(
            jnp.where((hit == 1) & (n_own == s), g, q) for s, q in enumerate(picks)
        )
        n_own = n_own + hit
        hit, _, within = find(g, sib_col)
        slot_sib[g] = jnp.where(hit == 1, jnp.minimum(n_sib, 6), 6)
        w_sib[g] = within
        n_sib = n_sib + hit
        rot[g] = find(g, row)[2]
        return n_own, n_sib, picks

    zero = jnp.int32(0)
    _, _, picks = lax.fori_loop(0, 16, table_g, (zero, zero, (zero,) * 6))
    for s in range(6):
        gsel[s] = picks[s]

    def piece(h, side, s0, s1, p):
        return lbuf[h].at[side, p, pl.ds(s0, s1 - s0)]

    def gather(h):
        out, into = [], []
        for n, (dz, s0, s1) in enumerate(((1, 0, 6), (-1, 0, 6), (2, 0, 3), (-2, 3, 6))):
            src = own.at[h, pl.ds(s0, s1 - s0)]
            sems = (g_send.at[h, n], g_recv.at[h, n])
            out.append(remote(src, piece(h, 0, s0, s1, part), *sems, at_z(dz)))
            p = (part - dz + 4) % 4
            into.append(remote(src, piece(h, 0, s0, s1, p), *sems, at_z(dz)))
        return out, into

    def forward(h):
        out = [
            remote(
                own.at[h], piece(h, 1, 0, 6, part), g_send.at[h, 4], g_recv.at[h, 4], sib
            )
        ]
        for n, (dz, s0, s1) in enumerate(((-1, 0, 6), (1, 0, 6), (-2, 0, 3), (2, 3, 6))):
            p = (part + dz + 4) % 4
            out.append(
                remote(
                    piece(h, 0, s0, s1, p), piece(h, 1, s0, s1, p),
                    g_send.at[h, 5 + n], g_recv.at[h, 5 + n], sib,
                )
            )
        return out

    gathers, gathered = zip(*[gather(h) for h in range(2)])
    forwards = [forward(h) for h in range(2)]
    for h in range(2):
        def land(n, _, h=h):
            a2a_in(h, n).wait_recv()
            return 0

        lax.fori_loop(1, 16, land, 0)
        rbuf[h][col] = sb[h, col]
        for s in range(6):
            own[h, s] = rbuf[h][gsel[s]]
        for cp in gathers[h]:
            cp.start()
        forwards[h][0].start()

    def finish_l(h):
        for n in range(4):
            gathered[h][n].wait_recv()
            forwards[h][1 + n].start()
        lbuf[h][0, part, pl.ds(0, 6)] = own[h]
        for cp in forwards[h]:
            cp.wait_recv()

    def compute(h, i):
        def body(n, _):
            g = (n // 4) * 8 + (n % 4) * 2 + k
            blk = (rot[g] + i) & 3
            mine = lbuf[h][0, :, slot_own[g]].reshape(256, 128)
            theirs = lbuf[h][1, :, slot_sib[g]].reshape(256, 128)
            acc = jnp.dot(a_own[w_own[g], blk], mine, preferred_element_type=F32)
            acc += jnp.dot(a_sib[w_sib[g], blk], theirs, preferred_element_type=F32)
            x_ref[h, i, n] = (-acc).astype(BF16)
            return 0

        lax.fori_loop(0, 8, body, 0)

    def xc(h, i, m, src, dst, dev):
        return remote(src, dst, x_send.at[h, i, m], x_recv.at[h, i, m], dev)

    def xf_copies(h, i):
        xr = x_ref.at[h, i]
        return dict(
            s1p=xc(h, i, 0, xr.at[x2], r1.at[h, i, 0], to_xp),
            s1m=xc(h, i, 1, xr.at[4 + x2], r1.at[h, i, 1], to_xm),
            a_p=xc(h, i, 2, xr.at[4 + xp], r2.at[h, i, 0, 1 - yl], to_xp),
            a_m=xc(h, i, 3, xr.at[xm], r2.at[h, i, 1, yl], to_xm),
            b_p=xc(h, i, 4, xs.at[h, i, 0], r2.at[h, i, 0, yl], to_xp),
            b_m=xc(h, i, 5, xs.at[h, i, 1], r2.at[h, i, 1, 1 - yl], to_xm),
            y=xc(h, i, 6, xs.at[h, i, 2], ry.at[h, i], to_y),
        )

    def yf_copies(h, i):
        j = i - 2
        xr = x_ref.at[h, i]
        out = {}
        for m, xx in enumerate((x2, xp, xm, x)):
            out["y%d" % m] = xc(h, i, m, xr.at[(1 - yl) * 4 + xx], ryf.at[h, j, m], to_y)
        yw, into = ys.at[h, j], rbx.at[h, j]
        out["s1p"] = xc(h, i, 4, yw.at[0], ra.at[h, j, 0], to_xp)
        out["s1m"] = xc(h, i, 5, yw.at[1], ra.at[h, j, 1], to_xm)
        out["a_p"] = xc(h, i, 6, yw.at[2], into.at[0, 1], to_xp)
        out["a_m"] = xc(h, i, 7, yw.at[3], into.at[1, 0], to_xm)
        out["b_p"] = xc(h, i, 8, yw.at[4], into.at[0, 0], to_xp)
        out["b_m"] = xc(h, i, 9, yw.at[5], into.at[1, 1], to_xm)
        return out

    cps = {}
    for h in range(2):
        for i in range(4):
            cps[h, i] = xf_copies(h, i) if i in XF else yf_copies(h, i)

    def add(*terms):
        total = terms[0].astype(F32)
        for t in terms[1:]:
            total = total + t.astype(F32)
        return total.astype(BF16)

    def xf1(h, i):
        for m in ("s1p", "s1m", "a_p", "a_m"):
            cps[h, i][m].start()

    def xf2(h, i):
        cp = cps[h, i]
        cp["s1p"].wait_recv()
        xs[h, i, 0] = add(x_ref[h, i, xp], r1[h, i, 0])
        cp["b_p"].start()
        cp["s1m"].wait_recv()
        xs[h, i, 1] = add(x_ref[h, i, 4 + xm], r1[h, i, 1])
        cp["b_m"].start()

    def xf3(h, i):
        cp = cps[h, i]
        for m in ("a_p", "a_m", "b_p", "b_m"):
            cp[m].wait_recv()
        o = 1 - yl
        xs[h, i, 2] = add(x_ref[h, i, o * 4 + x], r2[h, i, 0, 1], r2[h, i, 1, 1])
        cp["y"].start()

    def xf4(h, i):
        cps[h, i]["y"].wait_recv()
        fin[h, i] = add(x_ref[h, i, yl * 4 + x], r2[h, i, 0, 0], r2[h, i, 1, 0], ry[h, i])

    def yf1(h, i):
        for m in range(4):
            cps[h, i]["y%d" % m].start()

    lo, hi = pl.ds(0, 128), pl.ds(128, 128)

    def yf2(h, i):
        cp = cps[h, i]
        j, o = i - 2, yl * 4
        cp["y0"].wait_recv()
        ys[h, j, 0] = add(x_ref[h, i, o + x2, lo], ryf[h, j, 0, lo])
        cp["s1p"].start()
        ys[h, j, 1] = add(x_ref[h, i, o + x2, hi], ryf[h, j, 0, hi])
        cp["s1m"].start()
        cp["y1"].wait_recv()
        ys[h, j, 2] = add(x_ref[h, i, o + xp, hi], ryf[h, j, 1, hi])
        cp["a_p"].start()
        cp["y2"].wait_recv()
        ys[h, j, 3] = add(x_ref[h, i, o + xm, lo], ryf[h, j, 2, lo])
        cp["a_m"].start()

    def yf3(h, i):
        cp = cps[h, i]
        j, o = i - 2, yl * 4
        cp["s1p"].wait_recv()
        ys[h, j, 4] = add(x_ref[h, i, o + xp, lo], ryf[h, j, 1, lo], ra[h, j, 0])
        cp["b_p"].start()
        cp["s1m"].wait_recv()
        ys[h, j, 5] = add(x_ref[h, i, o + xm, hi], ryf[h, j, 2, hi], ra[h, j, 1])
        cp["b_m"].start()

    def yf4(h, i):
        cp = cps[h, i]
        j, o = i - 2, yl * 4
        for m in ("y3", "a_p", "a_m", "b_p", "b_m"):
            cp[m].wait_recv()
        for n, rows in enumerate((lo, hi)):
            fin[h, i, rows] = add(
                x_ref[h, i, o + x, rows], ryf[h, j, 3, rows], rbx[h, j, 0, n], rbx[h, j, 1, n]
            )

    def dcopy(n):
        to = (row + n) % 16
        return remote(
            cb.at[to], rd.at[row],
            d_send.at[0, n], d_recv.at[0, n], (to, col),
        )

    def dcopy_in(n):
        fr = (row - n + 16) % 16
        return remote(
            cb.at[fr], rd.at[fr],
            d_send.at[0, n], d_recv.at[0, n], (fr, col),
        )

    def ecopy(n):
        to = (row + n) % 16
        return remote(dpart, ro.at[row], d_send.at[1, n], d_recv.at[1, n], (to, col))

    def ecopy_in(n):
        fr = (row - n + 16) % 16
        return remote(
            dpart, ro.at[fr],
            d_send.at[1, n], d_recv.at[1, n], (fr, col),
        )

    def diag1():
        hit, j, _ = find(col, row)
        jr = jnp.where(hit == 1, j, 6)
        for h in range(2):
            cb[:, :, pl.ds(128 * h, 128)] = lax.dot_general(
                lin[jr], fin[h, 0], (((0,), (0,)), ((), ())), preferred_element_type=F32
            ).astype(BF16).reshape(16, 16, 128)

        def go(n, _):
            dcopy(n).start()
            return 0

        lax.fori_loop(1, 16, go, 0)

    def diag2():
        def landed(n, _):
            dcopy_in(n).wait_recv()
            return 0

        lax.fori_loop(1, 16, landed, 0)
        rd[row] = cb[row]
        total = rd[0].astype(F32)
        for n in range(1, 16):
            total = total + rd[n].astype(F32)
        dpart[...] = total.astype(BF16)

        def go(n, _):
            ecopy(n).start()
            return 0

        lax.fori_loop(1, 16, go, 0)

    def diag3():
        def landed(n, _):
            ecopy_in(n).wait_recv()
            return 0

        lax.fori_loop(1, 16, landed, 0)
        ro[row] = dpart[...]
        dsum[...] = ro[...].reshape(256, 256)

    finish_l(0)
    for w in range(4):
        ld_a[w].wait()
        cp_a[w].wait_recv()
    compute(0, 0)
    xf1(0, 0)
    compute(0, 2)
    yf1(0, 2)
    finish_l(1)
    compute(1, 0)
    xf1(1, 0)
    xf2(0, 0)
    compute(1, 2)
    yf1(1, 2)
    compute(0, 1)
    xf1(0, 1)
    xf2(1, 0)
    xf3(0, 0)
    yf2(0, 2)
    compute(1, 1)
    xf1(1, 1)
    compute(0, 3)
    yf1(0, 3)
    xf3(1, 0)
    compute(1, 3)
    yf1(1, 3)
    xf2(0, 1)
    xf4(0, 0)
    xf4(1, 0)
    diag1()
    yf3(0, 2)
    xf2(1, 1)
    yf2(1, 2)
    xf3(0, 1)
    yf3(1, 2)
    xf3(1, 1)
    yf2(0, 3)
    diag2()
    yf3(0, 3)
    yf2(1, 3)
    yf3(1, 3)
    for h in range(2):
        xf4(h, 1)
        yf4(h, 2)
    for h in range(2):
        yf4(h, 3)

    first = rot[col]
    for q in range(4):
        i = (q - first + 4) & 3
        for h in range(2):
            panel[pl.ds(256 * q, 256), pl.ds(128 * h, 128)] = fin[h, i]
    diag3()

    for cp in cp_a:
        cp.wait_send()
    for h in range(2):
        def sent(n, _, h=h):
            a2a(h, n).wait_send()
            return 0

        lax.fori_loop(1, 16, sent, 0)
        for cp in gathers[h] + forwards[h]:
            cp.wait_send()
        for i in range(4):
            for cp in cps[h, i].values():
                cp.wait_send()

    def gone(n, _):
        dcopy(n).wait_send()
        ecopy(n).wait_send()
        return 0

    lax.fori_loop(1, 16, gone, 0)


def per_device(ancestor, lblocks, lrows, dinv):
    vm = pltpu.VMEM
    dma = pltpu.SemaphoreType.DMA
    smem = lambda *s: pltpu.SMEM(s, jnp.int32)
    panel, dsum = pl.pallas_call(
        kernel,
        out_shape=(
            jax.ShapeDtypeStruct((1024, 256), BF16),
            jax.ShapeDtypeStruct((256, 256), BF16),
        ),
        in_specs=[
            pl.BlockSpec(memory_space=pltpu.SMEM),
            pl.BlockSpec(memory_space=pl.ANY),
            pl.BlockSpec(memory_space=pl.ANY),
        ],
        out_specs=(pl.BlockSpec(memory_space=pltpu.VMEM), pl.BlockSpec(memory_space=pltpu.VMEM)),
        scratch_shapes=[
            vm((7, 256, 256), BF16),
            vm((4, 4, 256, 256), BF16),
            vm((4, 4, 256, 256), BF16),
            vm((2, 4, 7, 64, 128), BF16),
            vm((2, 4, 7, 64, 128), BF16),
            vm((2, 6, 64, 128), BF16),
            vm((2, 16, 64, 128), BF16),
            vm((16, 64, 128), BF16),
            vm((16, 64, 128), BF16),
            vm((2, 4, 8, 256, 128), BF16),
            vm((2, 2, 3, 256, 128), BF16),
            vm((2, 2, 6, 128, 128), BF16),
            vm((2, 2, 2, 256, 128), BF16),
            vm((2, 2, 2, 2, 256, 128), BF16),
            vm((2, 2, 256, 128), BF16),
            vm((2, 2, 4, 256, 128), BF16),
            vm((2, 2, 2, 128, 128), BF16),
            vm((2, 2, 2, 2, 128, 128), BF16),
            vm((2, 4, 256, 128), BF16),
            vm((16, 16, 256), BF16),
            vm((16, 16, 256), BF16),
            vm((16, 256), BF16),
            vm((16, 16, 256), BF16),
            smem(16), smem(16), smem(16), smem(16), smem(16), smem(16), smem(6),
            dma((5,)), dma((4,)), dma((4,)),
            dma((2, 16)), dma((16,)), dma((16,)),
            dma((2, 9)), dma((2, 9)),
            dma((2, 4, 10)), dma((2, 4, 10)),
            dma((2, 16)), dma((2, 16)),
        ],
        compiler_params=pltpu.CompilerParams(
            collective_id=0, has_side_effects=True, vmem_limit_bytes=60 * 2**20
        ),
        name="panel",
    )(lrows.T, ancestor.reshape(4, 256, 1024), lblocks[0])
    return panel[None], dinv - dsum.astype(F32)[None]


def solution(mesh):
    return jax.shard_map(
        per_device,
        mesh=mesh,
        in_specs=(P("row", "col"), P("col", None, None, None), P(), P("col", None, None)),
        out_specs=(P("col", "row", None), P("col", None, None)),
        check_vma=False,
    )
```

```python
import functools

import jax
import jax.numpy as jnp
from jax import lax
from jax.experimental import pallas as pl
from jax.experimental.pallas import tpu as pltpu
from jax.sharding import PartitionSpec as P

MESH = pl.DeviceIdType.MESH
UNROLL = 2
F32 = jnp.float32
BF16 = jnp.bfloat16

XF = (0, 1)
YF = (2, 3)


def kernel(
    lrows, anc, lb, panel, dsum,
    lin, a_own, a_sib, l0, l1, own, sb, rb0, rb1,
    x_ref, xs, ys, r1, r2, ry, ryf, ra, rbx, fin, cb, rd, dpart, ro,
    jt, slot_own, w_own, slot_sib, w_sib, rot, gsel,
    loc_sem, a_send, a_recv, t_send, t_recv0, t_recv1, g_send, g_recv,
    x_send, x_recv, d_send, d_recv,
):
    row = lax.axis_index("row")
    col = lax.axis_index("col")
    yh, z = row // 8, row % 8
    yl, x, k = col // 8, (col // 2) % 4, col % 2
    part = z % 4
    lbuf = (l0, l1)
    rbuf = (rb0, rb1)
    t_recv = (t_recv0, t_recv1)

    def at_col(y_, x_, k_):
        return (row, y_ * 8 + x_ * 2 + k_)

    def at_z(dz):
        return (yh * 8 + (z + dz + 8) % 8, col)

    xp, xm, x2 = (x + 1) % 4, (x + 3) % 4, (x + 2) % 4
    sib = at_col(yl, x, 1 - k)
    to_y = at_col(1 - yl, x, k)
    to_xp = at_col(yl, xp, k)
    to_xm = at_col(yl, xm, k)

    def remote(src, dst, send, recv, dev):
        return pltpu.make_async_remote_copy(
            src_ref=src, dst_ref=dst, send_sem=send, recv_sem=recv,
            device_id=dev, device_id_type=MESH,
        )

    lin[6] = jnp.zeros((256, 256), BF16)
    for h in range(2):
        for s in range(2):
            lbuf[h][s, :, 6] = jnp.zeros((4, 64, 128), BF16)

    ld_l = pltpu.make_async_copy(lb, lin.at[pl.ds(0, 6)], loc_sem.at[0])
    ld_l.start()
    barrier = pltpu.get_barrier_semaphore()

    def greet(n, _):
        pl.semaphore_signal(barrier, inc=1, device_id=(row, (col + n) % 16), device_id_type=MESH)
        pl.semaphore_signal(barrier, inc=1, device_id=((row + n) % 16, col), device_id_type=MESH)
        return 0

    lax.fori_loop(1, 16, greet, 0)

    def find(g, owner):
        hit = jnp.int32(0)
        j_at = jnp.int32(0)
        within = jnp.int32(0)
        for j in range(6):
            v = lrows[j, g]
            eq = (v >> 2) == owner
            hit = jnp.where(eq, 1, hit)
            j_at = jnp.where(eq, j, j_at)
            within = jnp.where(eq, v & 3, within)
        return hit, j_at, within

    def table_j(c, _):
        jt[c] = find(col, c)[1]
        return 0

    lax.fori_loop(0, 16, table_j, 0)
    pl.semaphore_wait(barrier, 30)

    ld_l.wait()
    rows_p = pl.ds(pl.multiple_of(part * 64, 64), 64)

    def a2a(h, n):
        c = (col + n) % 16
        return remote(
            sb.at[h, c], rbuf[h].at[col], t_send.at[h, n], t_recv[h].at[n], (row, c)
        )

    def a2a_in(h, n):
        c = (col - n + 16) % 16
        return remote(
            sb.at[h, c], rbuf[h].at[c], t_send.at[h, n], t_recv[h].at[n], (row, c)
        )

    def a2a_go(h):
        def pick(c, _):
            sb[h, c] = lin[jt[c], rows_p, pl.ds(128 * h, 128)]
            return 0

        lax.fori_loop(0, 16, pick, 0)

        def send(n, _):
            a2a(h, n).start()
            return 0

        lax.fori_loop(1, 16, send, 0)

    a2a_go(0)

    ld_a = []
    for w in range(4):
        cp = pltpu.make_async_copy(
            anc.at[:, :, pl.ds(256 * w, 256)], a_own.at[w], loc_sem.at[1 + w]
        )
        cp.start()
        ld_a.append(cp)

    cp_a = []
    for w in range(4):
        cp = remote(
            anc.at[:, :, pl.ds(256 * w, 256)], a_sib.at[w], a_send.at[w], a_recv.at[w], sib
        )
        cp.start()
        cp_a.append(cp)

    sib_col = col + 1 - 2 * k

    def table_g(g, carry):
        n_own, n_sib, picks = carry
        hit, _, within = find(g, col)
        slot_own[g] = jnp.where(hit == 1, jnp.minimum(n_own, 6), 6)
        w_own[g] = within
        picks = tuple(
            jnp.where((hit == 1) & (n_own == s), g, q) for s, q in enumerate(picks)
        )
        n_own = n_own + hit
        hit, _, within = find(g, sib_col)
        slot_sib[g] = jnp.where(hit == 1, jnp.minimum(n_sib, 6), 6)
        w_sib[g] = within
        n_sib = n_sib + hit
        rot[g] = find(g, row)[2]
        return n_own, n_sib, picks

    zero = jnp.int32(0)
    _, _, picks = lax.fori_loop(0, 16, table_g, (zero, zero, (zero,) * 6))
    for s in range(6):
        gsel[s] = picks[s]

    def piece(h, side, s0, s1, p):
        return lbuf[h].at[side, p, pl.ds(s0, s1 - s0)]

    def gather(h):
        out, into = [], []
        for n, (dz, s0, s1) in enumerate(((1, 0, 6), (-1, 0, 6), (2, 0, 3), (-2, 3, 6))):
            src = own.at[h, pl.ds(s0, s1 - s0)]
            sems = (g_send.at[h, n], g_recv.at[h, n])
            out.append(remote(src, piece(h, 0, s0, s1, part), *sems, at_z(dz)))
            p = (part - dz + 4) % 4
            into.append(remote(src, piece(h, 0, s0, s1, p), *sems, at_z(dz)))
        return out, into

    def forward(h):
        out = [
            remote(
                own.at[h], piece(h, 1, 0, 6, part), g_send.at[h, 4], g_recv.at[h, 4], sib
            )
        ]
        for n, (dz, s0, s1) in enumerate(((-1, 0, 6), (1, 0, 6), (-2, 0, 3), (2, 3, 6))):
            p = (part + dz + 4) % 4
            out.append(
                remote(
                    piece(h, 0, s0, s1, p), piece(h, 1, s0, s1, p),
                    g_send.at[h, 5 + n], g_recv.at[h, 5 + n], sib,
                )
            )
        return out

    gathers, gathered = zip(*[gather(h) for h in range(2)])
    forwards = [forward(h) for h in range(2)]
    for h in range(2):
        def land(n, _, h=h):
            a2a_in(h, n).wait_recv()
            return 0

        lax.fori_loop(1, 16, land, 0)
        rbuf[h][col] = sb[h, col]
        for s in range(6):
            own[h, s] = rbuf[h][gsel[s]]
        for cp in gathers[h]:
            cp.start()
        forwards[h][0].start()
        if h == 0:
            a2a_go(1)

    def finish_l(h):
        for n in range(4):
            gathered[h][n].wait_recv()
            forwards[h][1 + n].start()
        lbuf[h][0, part, pl.ds(0, 6)] = own[h]
        for cp in forwards[h]:
            cp.wait_recv()

    def compute(h, *blocks):
        def body(n, _):
            g = (n // 4) * 8 + (n % 4) * 2 + k
            first, w0, w1 = rot[g], w_own[g], w_sib[g]
            mine = lbuf[h][0, :, slot_own[g]].reshape(256, 128)
            theirs = lbuf[h][1, :, slot_sib[g]].reshape(256, 128)
            for i in blocks or range(4):
                blk = (first + i) & 3
                acc = jnp.dot(a_own[w0, blk], mine, preferred_element_type=F32)
                acc += jnp.dot(a_sib[w1, blk], theirs, preferred_element_type=F32)
                x_ref[h, i, n] = (-acc).astype(BF16)
            return 0

        lax.fori_loop(0, 8, body, 0, unroll=UNROLL)

    def xc(h, i, m, src, dst, dev):
        return remote(src, dst, x_send.at[h, i, m], x_recv.at[h, i, m], dev)

    def xf_copies(h, i):
        xr = x_ref.at[h, i]
        return dict(
            s1p=xc(h, i, 0, xr.at[x2], r1.at[h, i, 0], to_xp),
            s1m=xc(h, i, 1, xr.at[4 + x2], r1.at[h, i, 1], to_xm),
            a_p=xc(h, i, 2, xr.at[4 + xp], r2.at[h, i, 0, 1 - yl], to_xp),
            a_m=xc(h, i, 3, xr.at[xm], r2.at[h, i, 1, yl], to_xm),
            b_p=xc(h, i, 4, xs.at[h, i, 0], r2.at[h, i, 0, yl], to_xp),
            b_m=xc(h, i, 5, xs.at[h, i, 1], r2.at[h, i, 1, 1 - yl], to_xm),
            y=xc(h, i, 6, xs.at[h, i, 2], ry.at[h, i], to_y),
        )

    def yf_copies(h, i):
        j = i - 2
        xr = x_ref.at[h, i]
        out = {}
        for m, xx in enumerate((x2, xp, xm, x)):
            out["y%d" % m] = xc(h, i, m, xr.at[(1 - yl) * 4 + xx], ryf.at[h, j, m], to_y)
        yw, into = ys.at[h, j], rbx.at[h, j]
        out["s1p"] = xc(h, i, 4, yw.at[0], ra.at[h, j, 0], to_xp)
        out["s1m"] = xc(h, i, 5, yw.at[1], ra.at[h, j, 1], to_xm)
        out["a_p"] = xc(h, i, 6, yw.at[2], into.at[0, 1], to_xp)
        out["a_m"] = xc(h, i, 7, yw.at[3], into.at[1, 0], to_xm)
        out["b_p"] = xc(h, i, 8, yw.at[4], into.at[0, 0], to_xp)
        out["b_m"] = xc(h, i, 9, yw.at[5], into.at[1, 1], to_xm)
        return out

    cps = {}
    for h in range(2):
        for i in range(4):
            cps[h, i] = xf_copies(h, i) if i in XF else yf_copies(h, i)

    def add(*terms):
        total = terms[0].astype(F32)
        for t in terms[1:]:
            total = total + t.astype(F32)
        return total.astype(BF16)

    def S(h, i):
        for m in ("s1p", "s1m"):
            cps[h, i][m].start()

    def A(h, i):
        for m in ("a_p", "a_m"):
            cps[h, i][m].start()

    def B(h, i):
        cp = cps[h, i]
        cp["s1p"].wait_recv()
        xs[h, i, 0] = add(x_ref[h, i, xp], r1[h, i, 0])
        cp["b_p"].start()
        cp["s1m"].wait_recv()
        xs[h, i, 1] = add(x_ref[h, i, 4 + xm], r1[h, i, 1])
        cp["b_m"].start()

    def T(h, i):
        cp = cps[h, i]
        for m in ("a_p", "a_m", "b_p", "b_m"):
            cp[m].wait_recv()
        o = 1 - yl
        xs[h, i, 2] = add(x_ref[h, i, o * 4 + x], r2[h, i, 0, 1], r2[h, i, 1, 1])
        cp["y"].start()

    def F(h, i):
        cps[h, i]["y"].wait_recv()
        fin[h, i] = add(x_ref[h, i, yl * 4 + x], r2[h, i, 0, 0], r2[h, i, 1, 0], ry[h, i])

    def Y(h, i, *which):
        for m in which or range(4):
            cps[h, i]["y%d" % m].start()

    lo, hi = pl.ds(0, 128), pl.ds(128, 128)

    def XS(h, i):
        cp = cps[h, i]
        j, o = i - 2, yl * 4
        cp["y0"].wait_recv()
        ys[h, j, 0] = add(x_ref[h, i, o + x2, lo], ryf[h, j, 0, lo])
        cp["s1p"].start()
        ys[h, j, 1] = add(x_ref[h, i, o + x2, hi], ryf[h, j, 0, hi])
        cp["s1m"].start()

    def XA(h, i):
        cp = cps[h, i]
        j, o = i - 2, yl * 4
        cp["y1"].wait_recv()
        ys[h, j, 2] = add(x_ref[h, i, o + xp, hi], ryf[h, j, 1, hi])
        cp["a_p"].start()
        cp["y2"].wait_recv()
        ys[h, j, 3] = add(x_ref[h, i, o + xm, lo], ryf[h, j, 2, lo])
        cp["a_m"].start()

    def XB(h, i):
        cp = cps[h, i]
        j, o = i - 2, yl * 4
        cp["s1p"].wait_recv()
        ys[h, j, 4] = add(x_ref[h, i, o + xp, lo], ryf[h, j, 1, lo], ra[h, j, 0])
        cp["b_p"].start()
        cp["s1m"].wait_recv()
        ys[h, j, 5] = add(x_ref[h, i, o + xm, hi], ryf[h, j, 2, hi], ra[h, j, 1])
        cp["b_m"].start()

    def G(h, i):
        cp = cps[h, i]
        j, o = i - 2, yl * 4
        for m in ("y3", "a_p", "a_m", "b_p", "b_m"):
            cp[m].wait_recv()
        for n, rows in enumerate((lo, hi)):
            fin[h, i, rows] = add(
                x_ref[h, i, o + x, rows], ryf[h, j, 3, rows], rbx[h, j, 0, n], rbx[h, j, 1, n]
            )

    def dcopy(n):
        to = (row + n) % 16
        return remote(
            cb.at[to], rd.at[row],
            d_send.at[0, n], d_recv.at[0, n], (to, col),
        )

    def dcopy_in(n):
        fr = (row - n + 16) % 16
        return remote(
            cb.at[fr], rd.at[fr],
            d_send.at[0, n], d_recv.at[0, n], (fr, col),
        )

    def ecopy(n):
        to = (row + n) % 16
        return remote(dpart, ro.at[row], d_send.at[1, n], d_recv.at[1, n], (to, col))

    def ecopy_in(n):
        fr = (row - n + 16) % 16
        return remote(
            dpart, ro.at[fr],
            d_send.at[1, n], d_recv.at[1, n], (fr, col),
        )

    def diag1():
        hit, j, _ = find(col, row)
        jr = jnp.where(hit == 1, j, 6)
        for h in range(2):
            cb[:, :, pl.ds(128 * h, 128)] = lax.dot_general(
                lin[jr], fin[h, 0], (((0,), (0,)), ((), ())), preferred_element_type=F32
            ).astype(BF16).reshape(16, 16, 128)

        def go(n, _):
            dcopy(n).start()
            return 0

        lax.fori_loop(1, 16, go, 0)

    def diag2():
        def landed(n, _):
            dcopy_in(n).wait_recv()
            return 0

        lax.fori_loop(1, 16, landed, 0)
        rd[row] = cb[row]
        total = rd[0].astype(F32)
        for n in range(1, 16):
            total = total + rd[n].astype(F32)
        dpart[...] = total.astype(BF16)

        def go(n, _):
            ecopy(n).start()
            return 0

        lax.fori_loop(1, 16, go, 0)

    def diag3():
        def landed(n, _):
            ecopy_in(n).wait_recv()
            return 0

        lax.fori_loop(1, 16, landed, 0)
        ro[row] = dpart[...]
        dsum[...] = ro[...].reshape(256, 256)

    finish_l(0)
    for w in range(4):
        ld_a[w].wait()
        cp_a[w].wait_recv()
    compute(0, 0, 2)
    Y(0, 2)
    S(0, 0)
    A(0, 0)
    compute(0, 1, 3)
    S(0, 1)
    A(0, 1)
    finish_l(1)
    compute(1, 0, 2)
    Y(0, 3)
    S(1, 0)
    B(0, 0)
    B(0, 1)
    compute(1, 1, 3)
    XS(0, 2)
    XA(0, 2)
    A(1, 0)
    Y(1, 2)
    T(0, 0)
    B(1, 0)
    S(1, 1)
    A(1, 1)
    XB(0, 2)
    XS(0, 3)
    XA(0, 3)
    T(1, 0)
    F(0, 0)
    F(1, 0)
    diag1()
    Y(1, 3)
    T(0, 1)
    B(1, 1)
    XB(0, 3)
    XS(1, 2)
    XA(1, 2)
    XB(1, 2)
    T(1, 1)
    diag2()
    XS(1, 3)
    XA(1, 3)
    XB(1, 3)
    F(0, 1)
    F(1, 1)
    G(0, 2)
    G(0, 3)
    G(1, 2)
    G(1, 3)

    first = rot[col]
    for q in range(4):
        i = (q - first + 4) & 3
        for h in range(2):
            panel[pl.ds(256 * q, 256), pl.ds(128 * h, 128)] = fin[h, i]
    diag3()

    for cp in cp_a:
        cp.wait_send()
    for h in range(2):
        def sent(n, _, h=h):
            a2a(h, n).wait_send()
            return 0

        lax.fori_loop(1, 16, sent, 0)
        for cp in gathers[h] + forwards[h]:
            cp.wait_send()
        for i in range(4):
            for cp in cps[h, i].values():
                cp.wait_send()

    def gone(n, _):
        dcopy(n).wait_send()
        ecopy(n).wait_send()
        return 0

    lax.fori_loop(1, 16, gone, 0)


def per_device(ancestor, lblocks, lrows, dinv):
    vm = pltpu.VMEM
    dma = pltpu.SemaphoreType.DMA
    smem = lambda *s: pltpu.SMEM(s, jnp.int32)
    panel, dsum = pl.pallas_call(
        kernel,
        out_shape=(
            jax.ShapeDtypeStruct((1024, 256), BF16),
            jax.ShapeDtypeStruct((256, 256), BF16),
        ),
        in_specs=[
            pl.BlockSpec(memory_space=pltpu.SMEM),
            pl.BlockSpec(memory_space=pl.ANY),
            pl.BlockSpec(memory_space=pl.ANY),
        ],
        out_specs=(pl.BlockSpec(memory_space=pltpu.VMEM), pl.BlockSpec(memory_space=pltpu.VMEM)),
        scratch_shapes=[
            vm((7, 256, 256), BF16),
            vm((4, 4, 256, 256), BF16),
            vm((4, 4, 256, 256), BF16),
            vm((2, 4, 7, 64, 128), BF16),
            vm((2, 4, 7, 64, 128), BF16),
            vm((2, 6, 64, 128), BF16),
            vm((2, 16, 64, 128), BF16),
            vm((16, 64, 128), BF16),
            vm((16, 64, 128), BF16),
            vm((2, 4, 8, 256, 128), BF16),
            vm((2, 2, 3, 256, 128), BF16),
            vm((2, 2, 6, 128, 128), BF16),
            vm((2, 2, 2, 256, 128), BF16),
            vm((2, 2, 2, 2, 256, 128), BF16),
            vm((2, 2, 256, 128), BF16),
            vm((2, 2, 4, 256, 128), BF16),
            vm((2, 2, 2, 128, 128), BF16),
            vm((2, 2, 2, 2, 128, 128), BF16),
            vm((2, 4, 256, 128), BF16),
            vm((16, 16, 256), BF16),
            vm((16, 16, 256), BF16),
            vm((16, 256), BF16),
            vm((16, 16, 256), BF16),
            smem(16), smem(16), smem(16), smem(16), smem(16), smem(16), smem(6),
            dma((5,)), dma((4,)), dma((4,)),
            dma((2, 16)), dma((16,)), dma((16,)),
            dma((2, 9)), dma((2, 9)),
            dma((2, 4, 10)), dma((2, 4, 10)),
            dma((2, 16)), dma((2, 16)),
        ],
        compiler_params=pltpu.CompilerParams(
            collective_id=0, has_side_effects=True, vmem_limit_bytes=53 * 2**20
        ),
        name="panel",
    )(lrows.T, ancestor.reshape(4, 256, 1024), lblocks[0])
    return panel[None], dinv - dsum.astype(F32)[None]


def solution(mesh):
    return jax.shard_map(
        per_device,
        mesh=mesh,
        in_specs=(P("row", "col"), P("col", None, None, None), P(), P("col", None, None)),
        out_specs=(P("col", "row", None), P("col", None, None)),
        check_vma=False,
    )
```

```python
import functools

import jax
import jax.numpy as jnp
from jax import lax
from jax.experimental import pallas as pl
from jax.experimental.pallas import tpu as pltpu
from jax.sharding import PartitionSpec as P

MESH = pl.DeviceIdType.MESH
UNROLL = 4
DIRECT = ((1, 3),)
F32 = jnp.float32
BF16 = jnp.bfloat16

XF = (0, 1)
YF = (2, 3)


def kernel(
    lr_any, anc, lb, panel, dsum,
    lin, a_own, a_sib, l0, l1, own, sb, rb0, rb1,
    x_ref, xs, ys, r1, r2, ry, ryf, ra, rbx, fin, cb, rd, dpart, ro,
    lrows, jt, slot_own, w_own, slot_sib, w_sib, rot, gsel,
    loc_sem, a_send, a_recv, t_send, t_recv0, t_recv1, g_send, g_recv,
    x_send, x_recv, d_send, d_recv,
):
    row = lax.axis_index("row")
    col = lax.axis_index("col")
    yh, z = row // 8, row % 8
    yl, x, k = col // 8, (col // 2) % 4, col % 2
    part = z % 4
    lbuf = (l0, l1)
    rbuf = (rb0, rb1)
    t_recv = (t_recv0, t_recv1)

    def at_col(y_, x_, k_):
        return (row, y_ * 8 + x_ * 2 + k_)

    def at_z(dz):
        return (yh * 8 + (z + dz + 8) % 8, col)

    xp, xm, x2 = (x + 1) % 4, (x + 3) % 4, (x + 2) % 4
    sib = at_col(yl, x, 1 - k)
    to_y = at_col(1 - yl, x, k)
    to_xp = at_col(yl, xp, k)
    to_x2 = at_col(yl, x2, k)
    to_xm = at_col(yl, xm, k)

    def remote(src, dst, send, recv, dev):
        return pltpu.make_async_remote_copy(
            src_ref=src, dst_ref=dst, send_sem=send, recv_sem=recv,
            device_id=dev, device_id_type=MESH,
        )

    lin[6] = jnp.zeros((256, 256), BF16)
    for h in range(2):
        for s in range(2):
            lbuf[h][s, :, 6] = jnp.zeros((4, 64, 128), BF16)

    ld_r = pltpu.make_async_copy(lr_any, lrows, loc_sem.at[5])
    ld_r.start()
    ld_l = pltpu.make_async_copy(lb, lin.at[pl.ds(0, 6)], loc_sem.at[0])
    ld_l.start()
    barrier = pltpu.get_barrier_semaphore()

    def greet(n, _):
        pl.semaphore_signal(barrier, inc=1, device_id=(row, (col + n) % 16), device_id_type=MESH)
        pl.semaphore_signal(barrier, inc=1, device_id=((row + n) % 16, col), device_id_type=MESH)
        return 0

    lax.fori_loop(1, 16, greet, 0)

    ld_r.wait()

    def find(g, owner):
        hit = jnp.int32(0)
        j_at = jnp.int32(0)
        within = jnp.int32(0)
        for j in range(6):
            v = lrows[j, g]
            eq = (v >> 2) == owner
            hit = jnp.where(eq, 1, hit)
            j_at = jnp.where(eq, j, j_at)
            within = jnp.where(eq, v & 3, within)
        return hit, j_at, within

    def table_j(c, _):
        jt[c] = find(col, c)[1]
        return 0

    lax.fori_loop(0, 16, table_j, 0)
    pl.semaphore_wait(barrier, 30)

    ld_l.wait()
    rows_p = pl.ds(pl.multiple_of(part * 64, 64), 64)

    def a2a(h, n):
        c = (col + n) % 16
        return remote(
            sb.at[h, c], rbuf[h].at[col], t_send.at[h, n], t_recv[h].at[n], (row, c)
        )

    def a2a_in(h, n):
        c = (col - n + 16) % 16
        return remote(
            sb.at[h, c], rbuf[h].at[c], t_send.at[h, n], t_recv[h].at[n], (row, c)
        )

    def a2a_go(h):
        def pick(c, _):
            sb[h, c] = lin[jt[c], rows_p, pl.ds(128 * h, 128)]
            return 0

        lax.fori_loop(0, 16, pick, 0)

        def send(n, _):
            a2a(h, n).start()
            return 0

        lax.fori_loop(1, 16, send, 0)

    a2a_go(0)

    ld_a = []
    for w in range(4):
        cp = pltpu.make_async_copy(
            anc.at[:, :, pl.ds(256 * w, 256)], a_own.at[w], loc_sem.at[1 + w]
        )
        cp.start()
        ld_a.append(cp)

    sib_col = col + 1 - 2 * k

    def table_g(g, carry):
        n_own, n_sib, picks = carry
        hit, _, within = find(g, col)
        slot_own[g] = jnp.where(hit == 1, jnp.minimum(n_own, 6), 6)
        w_own[g] = within
        picks = tuple(
            jnp.where((hit == 1) & (n_own == s), g, q) for s, q in enumerate(picks)
        )
        n_own = n_own + hit
        hit, _, within = find(g, sib_col)
        slot_sib[g] = jnp.where(hit == 1, jnp.minimum(n_sib, 6), 6)
        w_sib[g] = within
        n_sib = n_sib + hit
        rot[g] = find(g, row)[2]
        return n_own, n_sib, picks

    zero = jnp.int32(0)
    _, _, picks = lax.fori_loop(0, 16, table_g, (zero, zero, (zero,) * 6))
    for s in range(6):
        gsel[s] = picks[s]

    def piece(h, side, s0, s1, p):
        return lbuf[h].at[side, p, pl.ds(s0, s1 - s0)]

    def gather(h):
        out, into = [], []
        for n, (dz, s0, s1) in enumerate(((1, 0, 6), (-1, 0, 6), (2, 0, 3), (-2, 3, 6))):
            src = own.at[h, pl.ds(s0, s1 - s0)]
            sems = (g_send.at[h, n], g_recv.at[h, n])
            out.append(remote(src, piece(h, 0, s0, s1, part), *sems, at_z(dz)))
            p = (part - dz + 4) % 4
            into.append(remote(src, piece(h, 0, s0, s1, p), *sems, at_z(dz)))
        return out, into

    def forward(h):
        out = [
            remote(
                own.at[h], piece(h, 1, 0, 6, part), g_send.at[h, 4], g_recv.at[h, 4], sib
            )
        ]
        for n, (dz, s0, s1) in enumerate(((-1, 0, 6), (1, 0, 6), (-2, 0, 3), (2, 3, 6))):
            p = (part + dz + 4) % 4
            out.append(
                remote(
                    piece(h, 0, s0, s1, p), piece(h, 1, s0, s1, p),
                    g_send.at[h, 5 + n], g_recv.at[h, 5 + n], sib,
                )
            )
        return out

    cp_a = [
        remote(
            anc.at[:, :, pl.ds(256 * w, 256)], a_sib.at[w], a_send.at[w], a_recv.at[w], sib
        )
        for w in range(4)
    ]

    gathers, gathered = zip(*[gather(h) for h in range(2)])
    forwards = [forward(h) for h in range(2)]
    for h in range(2):
        def land(n, _, h=h):
            a2a_in(h, n).wait_recv()
            return 0

        lax.fori_loop(1, 16, land, 0)
        rbuf[h][col] = sb[h, col]
        for s in range(6):
            own[h, s] = rbuf[h][gsel[s]]
        for cp in gathers[h]:
            cp.start()
        forwards[h][0].start()
        if h == 0:
            a2a_go(1)
            for cp in cp_a:
                cp.start()

    def finish_l(h):
        for n in range(4):
            gathered[h][n].wait_recv()
            forwards[h][1 + n].start()
        lbuf[h][0, part, pl.ds(0, 6)] = own[h]
        for cp in forwards[h]:
            cp.wait_recv()

    def compute(h, *blocks):
        def body(n, _):
            g = (n // 4) * 8 + (n % 4) * 2 + k
            first, w0, w1 = rot[g], w_own[g], w_sib[g]
            mine = lbuf[h][0, :, slot_own[g]].reshape(256, 128)
            theirs = lbuf[h][1, :, slot_sib[g]].reshape(256, 128)
            for i in blocks or range(4):
                blk = (first + i) & 3
                acc = jnp.dot(a_own[w0, blk], mine, preferred_element_type=F32)
                acc += jnp.dot(a_sib[w1, blk], theirs, preferred_element_type=F32)
                x_ref[h, i, n] = (-acc).astype(BF16)
            return 0

        lax.fori_loop(0, 8, body, 0, unroll=UNROLL)

    def xc(h, i, m, src, dst, dev):
        return remote(src, dst, x_send.at[h, i, m], x_recv.at[h, i, m], dev)

    def xf_copies(h, i):
        xr = x_ref.at[h, i]
        return dict(
            s1p=xc(h, i, 0, xr.at[x2], r1.at[h, i, 0], to_xp),
            s1m=xc(h, i, 1, xr.at[4 + x2], r1.at[h, i, 1], to_xm),
            a_p=xc(h, i, 2, xr.at[4 + xp], r2.at[h, i, 0, 1 - yl], to_xp),
            a_m=xc(h, i, 3, xr.at[xm], r2.at[h, i, 1, yl], to_xm),
            b_p=xc(h, i, 4, xs.at[h, i, 0], r2.at[h, i, 0, yl], to_xp),
            b_m=xc(h, i, 5, xs.at[h, i, 1], r2.at[h, i, 1, 1 - yl], to_xm),
            y=xc(h, i, 6, xs.at[h, i, 2], ry.at[h, i], to_y),
        )

    def yf_copies(h, i):
        j = i - 2
        xr = x_ref.at[h, i]
        out = {}
        for m, xx in enumerate((x2, xp, xm, x)):
            out["y%d" % m] = xc(h, i, m, xr.at[(1 - yl) * 4 + xx], ryf.at[h, j, m], to_y)
        yw, into = ys.at[h, j], rbx.at[h, j]
        out["s1p"] = xc(h, i, 4, yw.at[0], ra.at[h, j, 0], to_x2 if (h, i) in DIRECT else to_xp)
        out["s1m"] = xc(h, i, 5, yw.at[1], ra.at[h, j, 1], to_x2 if (h, i) in DIRECT else to_xm)
        out["a_p"] = xc(h, i, 6, yw.at[2], into.at[0, 1], to_xp)
        out["a_m"] = xc(h, i, 7, yw.at[3], into.at[1, 0], to_xm)
        out["b_p"] = xc(h, i, 8, yw.at[4], into.at[0, 0], to_xp)
        out["b_m"] = xc(h, i, 9, yw.at[5], into.at[1, 1], to_xm)
        return out

    cps = {}
    for h in range(2):
        for i in range(4):
            cps[h, i] = xf_copies(h, i) if i in XF else yf_copies(h, i)

    def add(*terms):
        total = terms[0].astype(F32)
        for t in terms[1:]:
            total = total + t.astype(F32)
        return total.astype(BF16)

    def S(h, i):
        for m in ("s1p", "s1m"):
            cps[h, i][m].start()

    def A(h, i):
        for m in ("a_p", "a_m"):
            cps[h, i][m].start()

    def B(h, i):
        cp = cps[h, i]
        cp["s1p"].wait_recv()
        xs[h, i, 0] = add(x_ref[h, i, xp], r1[h, i, 0])
        cp["b_p"].start()
        cp["s1m"].wait_recv()
        xs[h, i, 1] = add(x_ref[h, i, 4 + xm], r1[h, i, 1])
        cp["b_m"].start()

    def T(h, i):
        cp = cps[h, i]
        for m in ("a_p", "a_m", "b_p", "b_m"):
            cp[m].wait_recv()
        o = 1 - yl
        xs[h, i, 2] = add(x_ref[h, i, o * 4 + x], r2[h, i, 0, 1], r2[h, i, 1, 1])
        cp["y"].start()

    def F(h, i):
        cps[h, i]["y"].wait_recv()
        fin[h, i] = add(x_ref[h, i, yl * 4 + x], r2[h, i, 0, 0], r2[h, i, 1, 0], ry[h, i])

    def Y(h, i, *which):
        for m in which or range(4):
            cps[h, i]["y%d" % m].start()

    lo, hi = pl.ds(0, 128), pl.ds(128, 128)

    def XS(h, i):
        cp = cps[h, i]
        j, o = i - 2, yl * 4
        cp["y0"].wait_recv()
        ys[h, j, 0] = add(x_ref[h, i, o + x2, lo], ryf[h, j, 0, lo])
        cp["s1p"].start()
        ys[h, j, 1] = add(x_ref[h, i, o + x2, hi], ryf[h, j, 0, hi])
        cp["s1m"].start()

    def XA(h, i):
        cp = cps[h, i]
        j, o = i - 2, yl * 4
        cp["y1"].wait_recv()
        ys[h, j, 2] = add(x_ref[h, i, o + xp, hi], ryf[h, j, 1, hi])
        cp["a_p"].start()
        cp["y2"].wait_recv()
        ys[h, j, 3] = add(x_ref[h, i, o + xm, lo], ryf[h, j, 2, lo])
        cp["a_m"].start()

        if (h, i) in DIRECT:
            ys[h, j, 4] = add(x_ref[h, i, o + xp, lo], ryf[h, j, 1, lo])
            cp["b_p"].start()
            ys[h, j, 5] = add(x_ref[h, i, o + xm, hi], ryf[h, j, 2, hi])
            cp["b_m"].start()

    def XB(h, i):
        if (h, i) in DIRECT:
            return
        cp = cps[h, i]
        j, o = i - 2, yl * 4
        cp["s1p"].wait_recv()
        ys[h, j, 4] = add(x_ref[h, i, o + xp, lo], ryf[h, j, 1, lo], ra[h, j, 0])
        cp["b_p"].start()
        cp["s1m"].wait_recv()
        ys[h, j, 5] = add(x_ref[h, i, o + xm, hi], ryf[h, j, 2, hi], ra[h, j, 1])
        cp["b_m"].start()

    def G(h, i):
        cp = cps[h, i]
        j, o = i - 2, yl * 4
        for m in ("y3", "a_p", "a_m", "b_p", "b_m"):
            cp[m].wait_recv()
        if (h, i) in DIRECT:
            cp["s1p"].wait_recv()
            cp["s1m"].wait_recv()
        for n, rows in enumerate((lo, hi)):
            terms = [x_ref[h, i, o + x, rows], ryf[h, j, 3, rows], rbx[h, j, 0, n], rbx[h, j, 1, n]]
            if (h, i) in DIRECT:
                terms.append(ra[h, j, n])
            fin[h, i, rows] = add(*terms)

    def dcopy(n):
        to = (row + n) % 16
        return remote(
            cb.at[to], rd.at[row],
            d_send.at[0, n], d_recv.at[0, n], (to, col),
        )

    def dcopy_in(n):
        fr = (row - n + 16) % 16
        return remote(
            cb.at[fr], rd.at[fr],
            d_send.at[0, n], d_recv.at[0, n], (fr, col),
        )

    def ecopy(n):
        to = (row + n) % 16
        return remote(dpart, ro.at[row], d_send.at[1, n], d_recv.at[1, n], (to, col))

    def ecopy_in(n):
        fr = (row - n + 16) % 16
        return remote(
            dpart, ro.at[fr],
            d_send.at[1, n], d_recv.at[1, n], (fr, col),
        )

    def diag1():
        hit, j, _ = find(col, row)
        jr = jnp.where(hit == 1, j, 6)
        for h in range(2):
            cb[:, :, pl.ds(128 * h, 128)] = lax.dot_general(
                lin[jr], fin[h, 0], (((0,), (0,)), ((), ())), preferred_element_type=F32
            ).astype(BF16).reshape(16, 16, 128)

        def go(n, _):
            dcopy(n).start()
            return 0

        lax.fori_loop(1, 16, go, 0)

    def diag2():
        def landed(n, _):
            dcopy_in(n).wait_recv()
            return 0

        lax.fori_loop(1, 16, landed, 0)
        rd[row] = cb[row]
        total = rd[0].astype(F32)
        for n in range(1, 16):
            total = total + rd[n].astype(F32)
        dpart[...] = total.astype(BF16)

        def go(n, _):
            ecopy(n).start()
            return 0

        lax.fori_loop(1, 16, go, 0)

    def diag3():
        def landed(n, _):
            ecopy_in(n).wait_recv()
            return 0

        lax.fori_loop(1, 16, landed, 0)
        ro[row] = dpart[...]
        dsum[...] = ro[...].reshape(256, 256)

    finish_l(0)
    for w in range(4):
        ld_a[w].wait()
        cp_a[w].wait_recv()
    compute(0, 0, 2)
    Y(0, 2)
    S(0, 0)
    A(0, 0)
    compute(0, 1, 3)
    S(0, 1)
    A(0, 1)
    finish_l(1)
    compute(1, 0, 2)
    Y(0, 3)
    S(1, 0)
    B(0, 0)
    B(0, 1)
    compute(1, 1, 3)
    XS(0, 2)
    XA(0, 2)
    A(1, 0)
    Y(1, 2)
    T(0, 0)
    B(1, 0)
    S(1, 1)
    A(1, 1)
    XB(0, 2)
    XS(0, 3)
    XA(0, 3)
    T(1, 0)
    Y(1, 3, 0, 1)
    F(0, 0)
    F(1, 0)
    diag1()
    Y(1, 3, 2, 3)
    T(0, 1)
    B(1, 1)
    XB(0, 3)
    XS(1, 2)
    XA(1, 2)
    XB(1, 2)
    XS(1, 3)
    XA(1, 3)
    T(1, 1)
    diag2()
    F(0, 1)
    F(1, 1)
    G(0, 2)
    G(0, 3)
    G(1, 2)
    G(1, 3)

    first = rot[col]
    for q in range(4):
        i = (q - first + 4) & 3
        for h in range(2):
            panel[pl.ds(256 * q, 256), pl.ds(128 * h, 128)] = fin[h, i]
    diag3()

    for cp in cp_a:
        cp.wait_send()
    for h in range(2):
        def sent(n, _, h=h):
            a2a(h, n).wait_send()
            return 0

        lax.fori_loop(1, 16, sent, 0)
        for cp in gathers[h] + forwards[h]:
            cp.wait_send()
        for i in range(4):
            for cp in cps[h, i].values():
                cp.wait_send()

    def gone(n, _):
        dcopy(n).wait_send()
        ecopy(n).wait_send()
        return 0

    lax.fori_loop(1, 16, gone, 0)


def per_device(ancestor, lblocks, lrows, dinv):
    vm = pltpu.VMEM
    dma = pltpu.SemaphoreType.DMA
    smem = lambda *s: pltpu.SMEM(s, jnp.int32)
    panel, dsum = pl.pallas_call(
        kernel,
        out_shape=(
            jax.ShapeDtypeStruct((1024, 256), BF16),
            jax.ShapeDtypeStruct((256, 256), BF16),
        ),
        in_specs=[
            pl.BlockSpec(memory_space=pl.ANY),
            pl.BlockSpec(memory_space=pl.ANY),
            pl.BlockSpec(memory_space=pl.ANY),
        ],
        out_specs=(pl.BlockSpec(memory_space=pltpu.VMEM), pl.BlockSpec(memory_space=pltpu.VMEM)),
        scratch_shapes=[
            vm((7, 256, 256), BF16),
            vm((4, 4, 256, 256), BF16),
            vm((4, 4, 256, 256), BF16),
            vm((2, 4, 7, 64, 128), BF16),
            vm((2, 4, 7, 64, 128), BF16),
            vm((2, 6, 64, 128), BF16),
            vm((2, 16, 64, 128), BF16),
            vm((16, 64, 128), BF16),
            vm((16, 64, 128), BF16),
            vm((2, 4, 8, 256, 128), BF16),
            vm((2, 2, 3, 256, 128), BF16),
            vm((2, 2, 6, 128, 128), BF16),
            vm((2, 2, 2, 256, 128), BF16),
            vm((2, 2, 2, 2, 256, 128), BF16),
            vm((2, 2, 256, 128), BF16),
            vm((2, 2, 4, 256, 128), BF16),
            vm((2, 2, 2, 128, 128), BF16),
            vm((2, 2, 2, 2, 128, 128), BF16),
            vm((2, 4, 256, 128), BF16),
            vm((16, 16, 256), BF16),
            vm((16, 16, 256), BF16),
            vm((16, 256), BF16),
            vm((16, 16, 256), BF16),
            smem(6, 16), smem(16), smem(16), smem(16), smem(16), smem(16), smem(16), smem(6),
            dma((6,)), dma((4,)), dma((4,)),
            dma((2, 16)), dma((16,)), dma((16,)),
            dma((2, 9)), dma((2, 9)),
            dma((2, 4, 10)), dma((2, 4, 10)),
            dma((2, 16)), dma((2, 16)),
        ],
        compiler_params=pltpu.CompilerParams(
            collective_id=0, has_side_effects=True, vmem_limit_bytes=53 * 2**20
        ),
        name="panel",
    )(lrows.T, ancestor.reshape(4, 256, 1024), lblocks[0])
    return panel[None], dinv - dsum.astype(F32)[None]


def solution(mesh):
    return jax.shard_map(
        per_device,
        mesh=mesh,
        in_specs=(P("row", "col"), P("col", None, None, None), P(), P("col", None, None)),
        out_specs=(P("col", "row", None), P("col", None, None)),
        check_vma=False,
    )
```

```python
import functools

import jax
import jax.numpy as jnp
from jax import lax
from jax.experimental import pallas as pl
from jax.experimental.pallas import tpu as pltpu
from jax.sharding import PartitionSpec as P

MESH = pl.DeviceIdType.MESH
UNROLL = 4
DIRECT = ((1, 3),)
F32 = jnp.float32
BF16 = jnp.bfloat16

XF = (0, 1)
YF = (2, 3)


def kernel(
    lr_any, anc, lb, panel, dsum,
    lin, a_own, a_sib, l0, l1, own, sb, rb0, rb1,
    x_ref, xs, ys, r1, r2, ry, ryf, ra, rbx, fin, cb, rd, dpart, ro,
    lrows, jt, slot_own, w_own, slot_sib, w_sib, rot, gsel,
    loc_sem, a_send, a_recv, t_send, t_recv0, t_recv1, g_send, g_recv,
    x_send, x_recv, d_send, d_recv,
):
    row = lax.axis_index("row")
    col = lax.axis_index("col")
    yh, z = row // 8, row % 8
    yl, x, k = col // 8, (col // 2) % 4, col % 2
    part = z % 4
    lbuf = (l0, l1)
    rbuf = (rb0, rb1)
    t_recv = (t_recv0, t_recv1)

    def at_col(y_, x_, k_):
        return (row, y_ * 8 + x_ * 2 + k_)

    def at_z(dz):
        return (yh * 8 + (z + dz + 8) % 8, col)

    xp, xm, x2 = (x + 1) % 4, (x + 3) % 4, (x + 2) % 4
    sib = at_col(yl, x, 1 - k)
    to_y = at_col(1 - yl, x, k)
    to_xp = at_col(yl, xp, k)
    to_x2 = at_col(yl, x2, k)
    to_xm = at_col(yl, xm, k)

    def remote(src, dst, send, recv, dev):
        return pltpu.make_async_remote_copy(
            src_ref=src, dst_ref=dst, send_sem=send, recv_sem=recv,
            device_id=dev, device_id_type=MESH,
        )

    lin[6] = jnp.zeros((256, 256), BF16)
    for h in range(2):
        for s in range(2):
            lbuf[h][s, :, 6] = jnp.zeros((4, 64, 128), BF16)

    ld_r = pltpu.make_async_copy(lr_any, lrows, loc_sem.at[5])
    ld_r.start()
    ld_l = pltpu.make_async_copy(lb, lin.at[pl.ds(0, 6)], loc_sem.at[0])
    ld_l.start()
    barrier = pltpu.get_barrier_semaphore()

    def greet(n, _):
        pl.semaphore_signal(barrier, inc=1, device_id=(row, (col + n) % 16), device_id_type=MESH)
        pl.semaphore_signal(barrier, inc=1, device_id=((row + n) % 16, col), device_id_type=MESH)
        return 0

    lax.fori_loop(1, 16, greet, 0)

    ld_r.wait()

    def find(g, owner):
        hit = jnp.int32(0)
        j_at = jnp.int32(0)
        within = jnp.int32(0)
        for j in range(6):
            v = lrows[j, g]
            eq = (v >> 2) == owner
            hit = jnp.where(eq, 1, hit)
            j_at = jnp.where(eq, j, j_at)
            within = jnp.where(eq, v & 3, within)
        return hit, j_at, within

    def table_j(c, _):
        jt[c] = find(col, c)[1]
        return 0

    lax.fori_loop(0, 16, table_j, 0)
    pl.semaphore_wait(barrier, 30)

    ld_l.wait()
    rows_p = pl.ds(pl.multiple_of(part * 64, 64), 64)

    def a2a(h, n):
        c = (col + n) % 16
        return remote(
            sb.at[h, c], rbuf[h].at[col], t_send.at[h, n], t_recv[h].at[n], (row, c)
        )

    def a2a_in(h, n):
        c = (col - n + 16) % 16
        return remote(
            sb.at[h, c], rbuf[h].at[c], t_send.at[h, n], t_recv[h].at[n], (row, c)
        )

    def a2a_go(h):
        def pick(c, _):
            sb[h, c] = lin[jt[c], rows_p, pl.ds(128 * h, 128)]
            return 0

        lax.fori_loop(0, 16, pick, 0)

        def send(n, _):
            a2a(h, n).start()
            return 0

        lax.fori_loop(1, 16, send, 0)

    a2a_go(0)

    ld_a = []
    for w in range(4):
        cp = pltpu.make_async_copy(
            anc.at[:, :, pl.ds(256 * w, 256)], a_own.at[w], loc_sem.at[1 + w]
        )
        cp.start()
        ld_a.append(cp)

    sib_col = col + 1 - 2 * k

    def table_g(g, carry):
        n_own, n_sib, picks = carry
        hit, _, within = find(g, col)
        slot_own[g] = jnp.where(hit == 1, jnp.minimum(n_own, 6), 6)
        w_own[g] = within
        picks = tuple(
            jnp.where((hit == 1) & (n_own == s), g, q) for s, q in enumerate(picks)
        )
        n_own = n_own + hit
        hit, _, within = find(g, sib_col)
        slot_sib[g] = jnp.where(hit == 1, jnp.minimum(n_sib, 6), 6)
        w_sib[g] = within
        n_sib = n_sib + hit
        rot[g] = find(g, row)[2]
        return n_own, n_sib, picks

    zero = jnp.int32(0)
    _, _, picks = lax.fori_loop(0, 16, table_g, (zero, zero, (zero,) * 6))
    for s in range(6):
        gsel[s] = picks[s]

    def piece(h, side, s0, s1, p):
        return lbuf[h].at[side, p, pl.ds(s0, s1 - s0)]

    def gather(h):
        out, into = [], []
        for n, (dz, s0, s1) in enumerate(((1, 0, 6), (-1, 0, 6), (2, 0, 3), (-2, 3, 6))):
            src = own.at[h, pl.ds(s0, s1 - s0)]
            sems = (g_send.at[h, n], g_recv.at[h, n])
            out.append(remote(src, piece(h, 0, s0, s1, part), *sems, at_z(dz)))
            p = (part - dz + 4) % 4
            into.append(remote(src, piece(h, 0, s0, s1, p), *sems, at_z(dz)))
        return out, into

    def forward(h):
        out = [
            remote(
                own.at[h], piece(h, 1, 0, 6, part), g_send.at[h, 4], g_recv.at[h, 4], sib
            )
        ]
        for n, (dz, s0, s1) in enumerate(((-1, 0, 6), (1, 0, 6), (-2, 0, 3), (2, 3, 6))):
            p = (part + dz + 4) % 4
            out.append(
                remote(
                    piece(h, 0, s0, s1, p), piece(h, 1, s0, s1, p),
                    g_send.at[h, 5 + n], g_recv.at[h, 5 + n], sib,
                )
            )
        return out

    cp_a = [
        remote(
            anc.at[:, :, pl.ds(256 * w, 256)], a_sib.at[w], a_send.at[w], a_recv.at[w], sib
        )
        for w in range(4)
    ]

    gathers, gathered = zip(*[gather(h) for h in range(2)])
    forwards = [forward(h) for h in range(2)]
    for h in range(2):
        def land(n, _, h=h):
            a2a_in(h, n).wait_recv()
            return 0

        lax.fori_loop(1, 16, land, 0)
        rbuf[h][col] = sb[h, col]
        for s in range(6):
            own[h, s] = rbuf[h][gsel[s]]
        for cp in gathers[h]:
            cp.start()
        forwards[h][0].start()
        if h == 0:
            a2a_go(1)
            for cp in cp_a:
                cp.start()

    def finish_l(h):
        for n in range(4):
            gathered[h][n].wait_recv()
            forwards[h][1 + n].start()
        lbuf[h][0, part, pl.ds(0, 6)] = own[h]
        for cp in forwards[h]:
            cp.wait_recv()

    def compute(h, *blocks):
        def body(n, _):
            g = (n // 4) * 8 + (n % 4) * 2 + k
            first, w0, w1 = rot[g], w_own[g], w_sib[g]
            mine = lbuf[h][0, :, slot_own[g]].reshape(256, 128)
            theirs = lbuf[h][1, :, slot_sib[g]].reshape(256, 128)
            for i in blocks or range(4):
                blk = (first + i) & 3
                acc = jnp.dot(a_own[w0, blk], mine, preferred_element_type=F32)
                acc += jnp.dot(a_sib[w1, blk], theirs, preferred_element_type=F32)
                x_ref[h, i, n] = (-acc).astype(BF16)
            return 0

        lax.fori_loop(0, 8, body, 0, unroll=UNROLL)

    def xc(h, i, m, src, dst, dev):
        return remote(src, dst, x_send.at[h, i, m], x_recv.at[h, i, m], dev)

    def xf_copies(h, i):
        xr = x_ref.at[h, i]
        return dict(
            s1p=xc(h, i, 0, xr.at[x2], r1.at[h, i, 0], to_xp),
            s1m=xc(h, i, 1, xr.at[4 + x2], r1.at[h, i, 1], to_xm),
            a_p=xc(h, i, 2, xr.at[4 + xp], r2.at[h, i, 0, 1 - yl], to_xp),
            a_m=xc(h, i, 3, xr.at[xm], r2.at[h, i, 1, yl], to_xm),
            b_p=xc(h, i, 4, xs.at[h, i, 0], r2.at[h, i, 0, yl], to_xp),
            b_m=xc(h, i, 5, xs.at[h, i, 1], r2.at[h, i, 1, 1 - yl], to_xm),
            y=xc(h, i, 6, xs.at[h, i, 2], ry.at[h, i], to_y),
        )

    def yf_copies(h, i):
        j = i - 2
        xr = x_ref.at[h, i]
        out = {}
        for m, xx in enumerate((x2, xp, xm, x)):
            out["y%d" % m] = xc(h, i, m, xr.at[(1 - yl) * 4 + xx], ryf.at[h, j, m], to_y)
        yw, into = ys.at[h, j], rbx.at[h, j]
        out["s1p"] = xc(h, i, 4, yw.at[0], ra.at[h, j, 0], to_x2 if (h, i) in DIRECT else to_xp)
        out["s1m"] = xc(h, i, 5, yw.at[1], ra.at[h, j, 1], to_x2 if (h, i) in DIRECT else to_xm)
        out["a_p"] = xc(h, i, 6, yw.at[2], into.at[0, 1], to_xp)
        out["a_m"] = xc(h, i, 7, yw.at[3], into.at[1, 0], to_xm)
        out["b_p"] = xc(h, i, 8, yw.at[4], into.at[0, 0], to_xp)
        out["b_m"] = xc(h, i, 9, yw.at[5], into.at[1, 1], to_xm)
        return out

    cps = {}
    for h in range(2):
        for i in range(4):
            cps[h, i] = xf_copies(h, i) if i in XF else yf_copies(h, i)

    def add(*terms):
        total = terms[0].astype(F32)
        for t in terms[1:]:
            total = total + t.astype(F32)
        return total.astype(BF16)

    def S(h, i):
        for m in ("s1p", "s1m"):
            cps[h, i][m].start()

    def A(h, i):
        for m in ("a_p", "a_m"):
            cps[h, i][m].start()

    def B(h, i):
        cp = cps[h, i]
        cp["s1p"].wait_recv()
        xs[h, i, 0] = add(x_ref[h, i, xp], r1[h, i, 0])
        cp["b_p"].start()
        cp["s1m"].wait_recv()
        xs[h, i, 1] = add(x_ref[h, i, 4 + xm], r1[h, i, 1])
        cp["b_m"].start()

    def T(h, i):
        cp = cps[h, i]
        for m in ("a_p", "a_m", "b_p", "b_m"):
            cp[m].wait_recv()
        o = 1 - yl
        xs[h, i, 2] = add(x_ref[h, i, o * 4 + x], r2[h, i, 0, 1], r2[h, i, 1, 1])
        cp["y"].start()

    def F(h, i):
        cps[h, i]["y"].wait_recv()
        fin[h, i] = add(x_ref[h, i, yl * 4 + x], r2[h, i, 0, 0], r2[h, i, 1, 0], ry[h, i])

    def Y(h, i, *which):
        for m in which or range(4):
            cps[h, i]["y%d" % m].start()

    lo, hi = pl.ds(0, 128), pl.ds(128, 128)

    def XS(h, i):
        cp = cps[h, i]
        j, o = i - 2, yl * 4
        cp["y0"].wait_recv()
        ys[h, j, 0] = add(x_ref[h, i, o + x2, lo], ryf[h, j, 0, lo])
        cp["s1p"].start()
        ys[h, j, 1] = add(x_ref[h, i, o + x2, hi], ryf[h, j, 0, hi])
        cp["s1m"].start()

    def XA(h, i):
        cp = cps[h, i]
        j, o = i - 2, yl * 4
        cp["y1"].wait_recv()
        ys[h, j, 2] = add(x_ref[h, i, o + xp, hi], ryf[h, j, 1, hi])
        cp["a_p"].start()
        cp["y2"].wait_recv()
        ys[h, j, 3] = add(x_ref[h, i, o + xm, lo], ryf[h, j, 2, lo])
        cp["a_m"].start()

        if (h, i) in DIRECT:
            ys[h, j, 4] = add(x_ref[h, i, o + xp, lo], ryf[h, j, 1, lo])
            cp["b_p"].start()
            ys[h, j, 5] = add(x_ref[h, i, o + xm, hi], ryf[h, j, 2, hi])
            cp["b_m"].start()

    def XB(h, i):
        if (h, i) in DIRECT:
            return
        cp = cps[h, i]
        j, o = i - 2, yl * 4
        cp["s1p"].wait_recv()
        ys[h, j, 4] = add(x_ref[h, i, o + xp, lo], ryf[h, j, 1, lo], ra[h, j, 0])
        cp["b_p"].start()
        cp["s1m"].wait_recv()
        ys[h, j, 5] = add(x_ref[h, i, o + xm, hi], ryf[h, j, 2, hi], ra[h, j, 1])
        cp["b_m"].start()

    def G(h, i):
        cp = cps[h, i]
        j, o = i - 2, yl * 4
        for m in ("y3", "a_p", "a_m", "b_p", "b_m"):
            cp[m].wait_recv()
        if (h, i) in DIRECT:
            cp["s1p"].wait_recv()
            cp["s1m"].wait_recv()
        for n, rows in enumerate((lo, hi)):
            terms = [x_ref[h, i, o + x, rows], ryf[h, j, 3, rows], rbx[h, j, 0, n], rbx[h, j, 1, n]]
            if (h, i) in DIRECT:
                terms.append(ra[h, j, n])
            fin[h, i, rows] = add(*terms)

    def dcopy(n):
        to = (row + n) % 16
        return remote(
            cb.at[to], rd.at[row],
            d_send.at[0, n], d_recv.at[0, n], (to, col),
        )

    def dcopy_in(n):
        fr = (row - n + 16) % 16
        return remote(
            cb.at[fr], rd.at[fr],
            d_send.at[0, n], d_recv.at[0, n], (fr, col),
        )

    def ecopy(n):
        to = (row + n) % 16
        return remote(dpart, ro.at[row], d_send.at[1, n], d_recv.at[1, n], (to, col))

    def ecopy_in(n):
        fr = (row - n + 16) % 16
        return remote(
            dpart, ro.at[fr],
            d_send.at[1, n], d_recv.at[1, n], (fr, col),
        )

    def diag1():
        hit, j, _ = find(col, row)
        jr = jnp.where(hit == 1, j, 6)
        for h in range(2):
            cb[:, :, pl.ds(128 * h, 128)] = lax.dot_general(
                lin[jr], fin[h, 0], (((0,), (0,)), ((), ())), preferred_element_type=F32
            ).astype(BF16).reshape(16, 16, 128)

        def go(n, _):
            dcopy(n).start()
            return 0

        lax.fori_loop(1, 16, go, 0)

    def diag2():
        def landed(n, _):
            dcopy_in(n).wait_recv()
            return 0

        lax.fori_loop(1, 16, landed, 0)
        rd[row] = cb[row]
        total = rd[0].astype(F32)
        for n in range(1, 16):
            total = total + rd[n].astype(F32)
        dpart[...] = total.astype(BF16)

        def go(n, _):
            ecopy(n).start()
            return 0

        lax.fori_loop(1, 16, go, 0)

    def diag3():
        def landed(n, _):
            ecopy_in(n).wait_recv()
            return 0

        lax.fori_loop(1, 16, landed, 0)
        ro[row] = dpart[...]
        dsum[...] = ro[...].reshape(256, 256)

    finish_l(0)
    for w in range(4):
        ld_a[w].wait()
        cp_a[w].wait_recv()
    compute(0, 0, 2)
    Y(0, 2)
    S(0, 0)
    A(0, 0)
    compute(0, 1, 3)
    S(0, 1)
    A(0, 1)
    finish_l(1)
    compute(1, 0, 2)
    Y(0, 3)
    S(1, 0)
    B(0, 0)
    B(0, 1)
    compute(1, 1, 3)
    XS(0, 2)
    XA(0, 2)
    A(1, 0)
    Y(1, 2)
    T(0, 0)
    B(1, 0)
    S(1, 1)
    A(1, 1)
    XB(0, 2)
    XS(0, 3)
    XA(0, 3)
    T(1, 0)
    Y(1, 3, 0, 1)
    F(0, 0)
    F(1, 0)
    diag1()
    Y(1, 3, 2, 3)
    T(0, 1)
    B(1, 1)
    XB(0, 3)
    XS(1, 2)
    XA(1, 2)
    XB(1, 2)
    XS(1, 3)
    XA(1, 3)
    diag2()
    T(1, 1)
    F(0, 1)
    F(1, 1)
    G(0, 2)
    G(0, 3)
    G(1, 2)
    G(1, 3)

    first = rot[col]
    for q in range(4):
        i = (q - first + 4) & 3
        for h in range(2):
            panel[pl.ds(256 * q, 256), pl.ds(128 * h, 128)] = fin[h, i]
    diag3()

    for cp in cp_a:
        cp.wait_send()
    for h in range(2):
        def sent(n, _, h=h):
            a2a(h, n).wait_send()
            return 0

        lax.fori_loop(1, 16, sent, 0)
        for cp in gathers[h] + forwards[h]:
            cp.wait_send()
        for i in range(4):
            for cp in cps[h, i].values():
                cp.wait_send()

    def gone(n, _):
        dcopy(n).wait_send()
        ecopy(n).wait_send()
        return 0

    lax.fori_loop(1, 16, gone, 0)


def per_device(ancestor, lblocks, lrows, dinv):
    vm = pltpu.VMEM
    dma = pltpu.SemaphoreType.DMA
    smem = lambda *s: pltpu.SMEM(s, jnp.int32)
    panel, dsum = pl.pallas_call(
        kernel,
        out_shape=(
            jax.ShapeDtypeStruct((1024, 256), BF16),
            jax.ShapeDtypeStruct((256, 256), BF16),
        ),
        in_specs=[
            pl.BlockSpec(memory_space=pl.ANY),
            pl.BlockSpec(memory_space=pl.ANY),
            pl.BlockSpec(memory_space=pl.ANY),
        ],
        out_specs=(pl.BlockSpec(memory_space=pltpu.VMEM), pl.BlockSpec(memory_space=pltpu.VMEM)),
        scratch_shapes=[
            vm((7, 256, 256), BF16),
            vm((4, 4, 256, 256), BF16),
            vm((4, 4, 256, 256), BF16),
            vm((2, 4, 7, 64, 128), BF16),
            vm((2, 4, 7, 64, 128), BF16),
            vm((2, 6, 64, 128), BF16),
            vm((2, 16, 64, 128), BF16),
            vm((16, 64, 128), BF16),
            vm((16, 64, 128), BF16),
            vm((2, 4, 8, 256, 128), BF16),
            vm((2, 2, 3, 256, 128), BF16),
            vm((2, 2, 6, 128, 128), BF16),
            vm((2, 2, 2, 256, 128), BF16),
            vm((2, 2, 2, 2, 256, 128), BF16),
            vm((2, 2, 256, 128), BF16),
            vm((2, 2, 4, 256, 128), BF16),
            vm((2, 2, 2, 128, 128), BF16),
            vm((2, 2, 2, 2, 128, 128), BF16),
            vm((2, 4, 256, 128), BF16),
            vm((16, 16, 256), BF16),
            vm((16, 16, 256), BF16),
            vm((16, 256), BF16),
            vm((16, 16, 256), BF16),
            smem(6, 16), smem(16), smem(16), smem(16), smem(16), smem(16), smem(16), smem(6),
            dma((6,)), dma((4,)), dma((4,)),
            dma((2, 16)), dma((16,)), dma((16,)),
            dma((2, 9)), dma((2, 9)),
            dma((2, 4, 10)), dma((2, 4, 10)),
            dma((2, 16)), dma((2, 16)),
        ],
        compiler_params=pltpu.CompilerParams(
            collective_id=0, has_side_effects=True, vmem_limit_bytes=53 * 2**20
        ),
        name="panel",
    )(lrows.T, ancestor.reshape(4, 256, 1024), lblocks[0])
    return panel[None], dinv - dsum.astype(F32)[None]


def solution(mesh):
    return jax.shard_map(
        per_device,
        mesh=mesh,
        in_specs=(P("row", "col"), P("col", None, None, None), P(), P("col", None, None)),
        out_specs=(P("col", "row", None), P("col", None, None)),
        check_vma=False,
    )
```
